32 devices in a mesh: grp: 2 (over y), kb: 4 (over z), gb: 4 (over x, core).
Axes of the slice: x: 2, y: 2, z: 4, core: 2. Of those that a mesh axis runs over, the one named last changes fastest.
Arguments:
- amplitudes: float32 [4, 384, 16], P('grp', 'kb'), parts along dimension 0, may hold values from -6 to 6
- pulse_field: float32 [4], P('grp'), parts along dimension 0, may hold values from -2 to 2
- pair_density: bfloat16 [2, 384, 16, 2000], P(None, 'kb', None, 'gb'), may hold values from -6 to 6
- energies: float32 [384, 16], P('kb'), may hold values from 1 to 3
- dipoles: float32 [2, 384, 16], P(None, 'kb'), may hold values from -6 to 6
- coulomb: float32 [2000], P('gb'), may hold values from 0.5 to 2
- screened: float32 [16, 2000], P(None, 'gb'), may hold values from 0.5 to 2
- partners: int32 [384, 8], P('kb'), may hold values from 0 to 383, as said below
- shells: int32 [384, 8], P('kb'), may hold values from 0 to 15
- counts: int32 [384], P('kb'), may hold values from 1 to 8
Outputs:
- advanced: float32 [4, 384, 16], P('grp', 'kb'), parts along dimension 0
The draws below stay inside these ranges and needn't reach their ends.
There are 2 independent parts, one for each index of `grp`. The reference program is written for one: setup_inputs(seed, part) draws one part's arguments, and reference() takes and returns one part's arrays. A program takes and returns all parts, laid end to end along the dimension named above; an argument that names none is the same for every part. Nothing has to cross between parts.
Inputs may be any that keep to these rules, and one draw needn't show every extreme that they name: The partners of a k point of block b (k // 96 = b) lie in blocks b, b - 1, b + 1 and b + 2, modulo 4; the partners of the k points of one block name exactly 24 distinct k points of each of these four blocks, and the first slot alone already names all of them; the partners of one k point are distinct.
All inputs are finite; a program needn't handle non-finite values.
Results may differ from the reference program's by a relative error of at most 0.0042.
Values may be sent and summed in bfloat16 or wider, within the bound.
A program may use at most 64 MiB of HBM per device.

```python
import math
import jax
import jax.numpy as jnp
from jax import lax

NCV = 16
NG = 2000
NQ = 16
NPART = 8
K_DEV = 96
CAP = 24
K = 384
N_KB = 4


def draw_partners(key, part):
    key = jax.random.fold_in(key, 11)
    key_perm, key_mult = jax.random.split(key)
    perm_keys = jax.random.split(key_perm, N_KB * 4)
    chosen = jax.vmap(lambda subkey: jax.random.permutation(subkey, K_DEV))(perm_keys)[:, :CAP]
    chosen = chosen.reshape(N_KB, 4 * CAP).astype(jnp.int32)
    offsets = jnp.array([0, N_KB - 1, 1, N_KB // 2], jnp.int32)
    blocks = (jnp.arange(N_KB, dtype=jnp.int32)[:, None] + offsets[None, :]) % N_KB
    candidates = jnp.repeat(blocks, CAP, axis=1) * K_DEV + chosen
    strides = 2 * jax.random.randint(key_mult, (N_KB, K_DEV), 0, 2 * CAP) + 1
    columns = (jnp.arange(K_DEV, dtype=jnp.int32)[None, :, None] + jnp.arange(NPART, dtype=jnp.int32)[None, None, :] * strides[:, :, None]) % (4 * CAP)
    spread = jnp.broadcast_to(candidates[:, None, :], (N_KB, K_DEV, 4 * CAP))
    picked = jnp.take_along_axis(spread, columns, axis=2)
    return picked.reshape(N_KB * K_DEV, NPART).astype(jnp.int32)


def draw_counts(key, part):
    key = jax.random.fold_in(key, 12)
    key_vals, key_top, key_low = jax.random.split(key, 3)
    values = jax.random.randint(key_vals, (N_KB * K_DEV,), 1, NPART + 1)
    top_at = jax.random.randint(key_top, (), 0, N_KB * K_DEV)
    low_at = jax.random.randint(key_low, (), 0, N_KB * K_DEV)
    positions = jnp.arange(N_KB * K_DEV)
    values = jnp.where(positions == low_at, 1, values)
    values = jnp.where(positions == top_at, NPART, values)
    return values.astype(jnp.int32)


def set_ends(entries, key, low, high):
    place = [jax.random.randint(jax.random.fold_in(key, axis), (), 0, length) for axis, length in enumerate(entries.shape)]
    longest = entries.shape.index(max(entries.shape))
    next_to = place[:longest] + [(place[longest] + 1) % entries.shape[longest]] + place[longest + 1:]
    return entries.at[tuple(place)].set(low).at[tuple(next_to)].set(high)


def level_of(stream_key, extent, cuts, least, largest):
    def one(axis_at, shards_of):
        heights = jax.random.uniform(jax.random.fold_in(jax.random.fold_in(stream_key, 6), axis_at), (shards_of,), jnp.float32, least / len(cuts), largest / len(cuts))
        return jnp.repeat(jnp.exp(heights), extent[axis_at] // shards_of).reshape((-1,) + (1,) * (len(extent) - axis_at - 1))

    loudness = one(*cuts[0])
    for cut in cuts[1:]:
        loudness = loudness * one(*cut)
    return loudness


def noise(stream_key, shape, width, most, pieces=(), held_as=jnp.bfloat16):
    drawn = width * jax.random.normal(stream_key, shape, jnp.float32)
    if pieces:
        drawn = drawn * level_of(stream_key, shape, pieces, -0.22, 0.18)
    return jnp.clip(drawn, -most, most).astype(held_as)


def setup_inputs(seed: int = 0, part: int = 0) -> dict:
    streams_of = jax.random.split(jax.random.key(seed), 11)
    part_keys = jax.random.split(jax.random.fold_in(streams_of[10], part), 11)
    return {
        "amplitudes": noise(part_keys[0], (2, K, NCV), 1.0, 6.0, ((1, 4),), jnp.float32),
        "pulse_field": jnp.clip(jax.random.uniform(part_keys[1], (2,), jnp.float32, -2.0, 2.0), -2.0, 2.0),
        "pair_density": noise(streams_of[2], (2, K, NCV, NG), 1.0, 6.0, ((1, 4), (3, 4))),
        "energies": jnp.clip(1.0 + 2.0 * jax.random.uniform(streams_of[3], (K, NCV), jnp.float32) ** level_of(streams_of[3], (K, NCV), ((0, 4),), -0.2, 0.2), 1.0, 3.0),
        "dipoles": noise(streams_of[4], (2, K, NCV), 1.0, 6.0, ((1, 4),), jnp.float32),
        "coulomb": jnp.clip(jnp.exp(math.log(2.0) - 1.3862944 * jax.random.uniform(streams_of[5], (NG,), jnp.float32) ** level_of(streams_of[5], (NG,), ((0, 4),), -0.2, 0.2)), 0.5, 2.0),
        "screened": jnp.clip(jnp.exp(math.log(2.0) - 1.3862944 * jax.random.uniform(streams_of[6], (NQ, NG), jnp.float32) ** level_of(streams_of[6], (NQ, NG), ((1, 4),), -0.2, 0.2)), 0.5, 2.0),
        "partners": draw_partners(jax.random.fold_in(streams_of[10], 71), part),
        "shells": set_ends(jax.random.randint(streams_of[8], (K, NPART), 0, NQ), jax.random.fold_in(streams_of[8], 1), 0, NQ - 1).astype(jnp.int32),
        "counts": draw_counts(jax.random.fold_in(streams_of[10], 71), part),
    }


time_step = 0.25

def rounded(values):
    return lax.optimization_barrier(values.astype(jnp.bfloat16)).astype(jnp.float32)

def derivative(amps, efield, pair_density, energies, dipoles, coulomb, screened, partners, shells, counts):
    rounded_amp = rounded(amps)
    blocks_m = pair_density.reshape(2, N_KB, K_DEV, NCV, NG).transpose(1, 0, 2, 3, 4)
    blocks_x = rounded_amp.reshape(2, N_KB, K_DEV, NCV).transpose(1, 0, 2, 3)

    def densities(block_item):
        matrices = block_item[0].astype(jnp.float32)
        vectors = block_item[1]
        dens_real = jnp.einsum('kcg,kc->kg', matrices[0], vectors[0]) - jnp.einsum('kcg,kc->kg', matrices[1], vectors[1])
        dens_imag = jnp.einsum('kcg,kc->kg', matrices[0], vectors[1]) + jnp.einsum('kcg,kc->kg', matrices[1], vectors[0])
        return jnp.stack([dens_real, dens_imag])
    g_field = lax.map(densities, (blocks_m, blocks_x))
    g_field = g_field.transpose(1, 0, 2, 3).reshape(2, K, NG)
    totals = lax.optimization_barrier(jnp.sum(g_field, axis=1))
    sent_rows = rounded(g_field)
    live_mask = (jnp.arange(NPART)[None, :] < counts[:, None]).astype(jnp.float32)
    exchange_weight = 2.0 / math.sqrt(NCV * K_DEV * N_KB)
    direct_weight = 1.0 / math.sqrt(NCV * NPART)

    def project(block_item):
        matrix_block, partner_block, shell_block, live_block = block_item
        pulled = sent_rows[:, partner_block]
        weights = screened[shell_block] * live_block[:, :, None]
        summed = lax.optimization_barrier(jnp.sum(pulled * weights[None], axis=2))
        forcing = rounded(exchange_weight * coulomb[None, None, :] * totals[:, None, :] - direct_weight * summed)
        matrices = matrix_block.astype(jnp.float32)
        proj_real = jnp.einsum('kcg,kg->kc', matrices[0], forcing[0]) + jnp.einsum('kcg,kg->kc', matrices[1], forcing[1])
        proj_imag = jnp.einsum('kcg,kg->kc', matrices[0], forcing[1]) - jnp.einsum('kcg,kg->kc', matrices[1], forcing[0])
        return jnp.stack([proj_real, proj_imag]) / math.sqrt(NG)
    projection = lax.map(project, (blocks_m, partners.reshape(N_KB, K_DEV, NPART), shells.reshape(N_KB, K_DEV, NPART), live_mask.reshape(N_KB, K_DEV, NPART)))
    projection = projection.transpose(1, 0, 2, 3).reshape(2, K, NCV)
    deriv_real = energies * amps[1] + projection[1] - efield * dipoles[1]
    deriv_imag = -(energies * amps[0] + projection[0] - efield * dipoles[0])
    return jnp.stack([deriv_real, deriv_imag])

def reference(amplitudes, pulse_field, pair_density, energies, dipoles, coulomb, screened, partners, shells, counts):
    half = amplitudes + 0.5 * time_step * derivative(amplitudes, pulse_field[0], pair_density, energies, dipoles, coulomb, screened, partners, shells, counts)
    return amplitudes + time_step * derivative(half, pulse_field[1], pair_density, energies, dipoles, coulomb, screened, partners, shells, counts)
```

```python
import functools
import math

import jax
import jax.numpy as jnp
from jax import lax
from jax.experimental import pallas as pl
from jax.experimental.pallas import tpu as pltpu
from jax.sharding import PartitionSpec as P

CAP = 24
TIME_STEP = 0.25
LANES = 128
MESH = pl.DeviceIdType.MESH
F32 = jnp.float32
BF16 = jnp.bfloat16


def iota(shape, dim):
    return lax.broadcasted_iota(jnp.int32, shape, dim)


def nn(a, b):
    return lax.dot_general(a, b, (((1,), (0,)), ((), ())), preferred_element_type=F32)


def nt(a, b):
    return lax.dot_general(a, b, (((1,), (1,)), ((), ())), preferred_element_type=F32)


def each(lo, hi, fn):
    if hi - lo <= 8:
        for i in range(lo, hi):
            fn(i)
    else:
        lax.fori_loop(lo, hi, lambda i, c: (fn(i), c)[1], 0)


def picks(rows4):
    wanted = jnp.concatenate(rows4 + rows4, axis=0)
    upper = (iota((LANES, LANES), 0) <= iota((LANES, LANES), 1)).astype(F32).astype(BF16)
    rank = nn(wanted.astype(BF16), upper)
    order = iota((2 * CAP, LANES), 0)
    order = jnp.where(order >= CAP, order - CAP, order).astype(F32) + 1.0
    blocks = []
    for s in range(4):
        hit = (rank[s : s + 1] == order).astype(F32) * wanted[s : s + 1]
        blocks.append(hit)
    return jnp.concatenate(blocks, axis=0)


def kernel(
    n_kb, n_gb, k_rows, pairs, slots, g_local, chunks, scales,
    pulse, state, dens_hbm, coulomb, screened, partners, shells, counts,
    out,
    dens, req_send, req_recv, zb, send, rows, nbuf, ybuf, onehot, weight, scr, coul,
    dens_sem, req_ssem, req_rsem, row_ssem, row_rsem, n_ssem, n_rsem, y_ssem, y_rsem,
):
    exchange_weight, direct_weight, g_scale = scales
    me = lax.axis_index("kb")
    mine = lax.axis_index("gb")
    groups = k_rows * pairs // 256
    per = 256 // pairs
    step = 2
    loads = []
    for i in range(groups // step):
        span = pl.ds(i * step * per, step * per)
        cp = pltpu.make_async_copy(dens_hbm.at[:, span], dens.at[:, span], dens_sem.at[i])
        cp.start()
        loads.append(cp)

    barrier = pltpu.get_barrier_semaphore()

    def greet_kb(i):
        pl.semaphore_signal(barrier, inc=1, device_id={"kb": lax.rem(me + i, n_kb)}, device_id_type=MESH)

    def greet_gb(i):
        pl.semaphore_signal(barrier, inc=1, device_id={"gb": lax.rem(mine + i, n_gb)}, device_id_type=MESH)

    each(1, n_kb, greet_kb)
    each(1, n_gb, greet_gb)

    span = n_kb * k_rows
    rel = partners[...] - me * k_rows
    rel = jnp.where(rel < 0, rel + span, rel)
    half_at = (n_kb // 2) * k_rows
    last_at = (n_kb - 1) * k_rows
    key = jnp.where(
        rel < k_rows,
        rel,
        jnp.where(
            rel >= last_at,
            rel - last_at + LANES,
            jnp.where(rel < 2 * k_rows, rel - k_rows + 2 * LANES, rel - half_at + 3 * LANES),
        ),
    )
    first = key[:, 0:1]
    mine4 = []
    for s in range(4):
        hit = (first == iota((k_rows, LANES), 1) + s * LANES).astype(F32)
        mine4.append(jnp.max(hit, axis=0, keepdims=True))
    for s in range(1, 4):
        req_send[s - 1] = jnp.broadcast_to(mine4[s], (8, LANES))

    pl.semaphore_wait(barrier, n_kb - 1 + n_gb - 1)

    sources = [None, lax.rem(me + n_kb - 1, n_kb), lax.rem(me + 1, n_kb), lax.rem(me + n_kb // 2, n_kb)]
    targets = [None, lax.rem(me + 1, n_kb), lax.rem(me + n_kb - 1, n_kb), lax.rem(me + n_kb // 2, n_kb)]
    reqs = []
    for s in range(1, 4):
        cp = pltpu.make_async_remote_copy(
            req_send.at[s - 1], req_recv.at[s - 1], req_ssem.at[s - 1], req_rsem.at[s - 1],
            device_id={"kb": sources[s]}, device_id_type=MESH,
        )
        cp.start()
        reqs.append(cp)

    own = picks(mine4)
    cols = 8 * CAP
    number = iota((8, LANES), 1).astype(F32).astype(BF16)
    at = iota((1, cols), 1)
    slot_at = (at >= 2 * CAP).astype(jnp.int32) + (at >= 4 * CAP).astype(jnp.int32) + (at >= 6 * CAP).astype(jnp.int32)
    imag_at = (at - slot_at * 2 * CAP >= CAP).astype(jnp.int32)
    wanted_key = nt(number, own.astype(BF16))[0:1].astype(jnp.int32) + slot_at * LANES
    scr[...] = jnp.zeros_like(scr)
    scr[:, 0:g_local] = screened[...]
    coul[...] = jnp.zeros_like(coul)
    coul[:, 0:g_local] = coulomb[...] * exchange_weight
    zb[...] = jnp.zeros_like(zb)
    hi = scr[...].astype(BF16)
    rest = scr[...] - hi.astype(F32)
    mid = rest.astype(BF16)
    low = (rest - mid.astype(F32)).astype(BF16)
    kinds = screened.shape[0]
    for j in range(slots):
        hit = key[:, j : j + 1] == wanted_key
        onehot[j * 2 * k_rows : j * 2 * k_rows + k_rows] = (
            jnp.where(imag_at == 0, hit.astype(F32), 0.0).astype(BF16)
        )
        onehot[j * 2 * k_rows + k_rows : (j + 1) * 2 * k_rows] = (
            jnp.where(imag_at == 1, hit.astype(F32), 0.0).astype(BF16)
        )
        kind = (shells[:, j : j + 1] == iota((k_rows, kinds), 1)).astype(F32)
        kind = jnp.where(counts[...] > j, kind, 0.0).astype(BF16)
        weight[j] = nn(kind, hi) + (nn(kind, mid) + nn(kind, low))

    for cp in reqs:
        cp.wait()
    given = picks([mine4[0]] + [req_recv[s][0:1] for s in range(3)])
    row_at = iota((cols, 1), 0)
    row_slot = (row_at >= 2 * CAP).astype(jnp.int32) + (row_at >= 4 * CAP).astype(jnp.int32) + (row_at >= 6 * CAP).astype(jnp.int32)
    row_imag = row_at - row_slot * 2 * CAP >= CAP
    choose = jnp.concatenate(
        [jnp.where(row_imag, 0.0, given), jnp.where(row_imag, given, 0.0)], axis=1
    ).astype(BF16)

    diag = iota((per, 256), 1) // pairs == iota((per, 256), 0)
    starts = [sum(chunks[:i]) for i in range(len(chunks))]

    def section(t, ar, ai):
        left, right = [], []
        for g in range(groups):
            br = jnp.where(diag, jnp.broadcast_to(ar[g : g + 1], (per, 256)), 0.0).astype(BF16)
            bi = jnp.where(diag, jnp.broadcast_to(ai[g : g + 1], (per, 256)), 0.0).astype(BF16)
            left.append(jnp.concatenate([br, bi], axis=0))
            right.append(jnp.concatenate([-bi, br], axis=0))
        row_copies = []
        n_copies = []
        for c, width in enumerate(chunks):
            lo = starts[c]
            real = min(width, g_local - lo)
            sr = jnp.zeros((1, real), F32)
            si = jnp.zeros((1, real), F32)
            for g in range(groups):
                if t == 0 and c == 0 and g % step == 0:
                    loads[g // step].wait()
                mr = dens[0, g * per : (g + 1) * per, :, lo : lo + real].reshape(256, real)
                mi = dens[1, g * per : (g + 1) * per, :, lo : lo + real].reshape(256, real)
                z = nn(left[g], mr) + nn(right[g], mi)
                sr = sr + jnp.sum(z[0:per], axis=0, keepdims=True)
                si = si + jnp.sum(z[per : 2 * per], axis=0, keepdims=True)
                zb[t, g * per : (g + 1) * per, lo : lo + real] = z[0:per].astype(BF16)
                zb[t, LANES + g * per : LANES + (g + 1) * per, lo : lo + real] = z[per : 2 * per].astype(BF16)
            if real < width:
                nbuf[t, c, pl.ds(me, 1)] = jnp.zeros((1, 2, width), F32)
            nbuf[t, c, pl.ds(me, 1), :, 0:real] = jnp.concatenate([sr, si], axis=0)[None]

            def n_copy(i, c=c):
                return pltpu.make_async_remote_copy(
                    nbuf.at[t, c, me], nbuf.at[t, c, me], n_ssem.at[t, c, i], n_rsem.at[t, c, i],
                    device_id={"kb": lax.rem(me + i, n_kb)}, device_id_type=MESH,
                )

            each(1, n_kb, lambda i: n_copy(i).start())
            n_copies.append(n_copy)
            picked = nn(choose, zb[t, :, lo : lo + width]).astype(BF16)
            started = []
            for s in range(1, 4):
                send[t, c, s - 1] = picked[s * 2 * CAP : (s + 1) * 2 * CAP]
            for s in (3, 1, 2):
                cp = pltpu.make_async_remote_copy(
                    send.at[t, c, s - 1], rows.at[t, c, s], row_ssem.at[t, c, s - 1], row_rsem.at[t, c, s - 1],
                    device_id={"kb": targets[s]}, device_id_type=MESH,
                )
                cp.start()
                started.append(cp)
            rows[t, c, 0] = picked[0 : 2 * CAP]
            row_copies.append(started)

        forces = []
        for c, width in enumerate(chunks):
            lo = starts[c]
            for cp in row_copies[c]:
                cp.wait()
            pulled = nn(onehot[...], rows[t, c].reshape(cols, width))
            sum_r = jnp.zeros((k_rows, width), F32)
            sum_i = jnp.zeros((k_rows, width), F32)
            for j in range(slots):
                w = weight[j, :, lo : lo + width]
                sum_r = sum_r + pulled[j * 2 * k_rows : j * 2 * k_rows + k_rows] * w
                sum_i = sum_i + pulled[j * 2 * k_rows + k_rows : (j + 1) * 2 * k_rows] * w
            each(1, n_kb, lambda i: n_copies[c](i).wait())
            total = lax.fori_loop(0, n_kb, lambda i, a: a + nbuf[t, c, i], jnp.zeros((2, width), F32))
            total = total * coul[:, lo : lo + width]
            forces.append(
                (
                    (total[0:1] - direct_weight * sum_r).astype(BF16),
                    (total[1:2] - direct_weight * sum_i).astype(BF16),
                )
            )

        for g in range(groups):
            y = jnp.zeros((2 * per, 256), F32)
            for c, width in enumerate(chunks):
                lo = starts[c]
                real = min(width, g_local - lo)
                fr = forces[c][0][g * per : (g + 1) * per, 0:real]
                fi = forces[c][1][g * per : (g + 1) * per, 0:real]
                mr = dens[0, g * per : (g + 1) * per, :, lo : lo + real].reshape(256, real)
                mi = dens[1, g * per : (g + 1) * per, :, lo : lo + real].reshape(256, real)
                y = y + nt(jnp.concatenate([fr, fi], axis=0), mr) + nt(jnp.concatenate([fi, -fr], axis=0), mi)
            yr = jnp.sum(jnp.where(diag, y[0:per], 0.0), axis=0, keepdims=True)
            yi = jnp.sum(jnp.where(diag, y[per : 2 * per], 0.0), axis=0, keepdims=True)
            ybuf[t, pl.ds(mine, 1), 0, g : g + 1] = yr[None]
            ybuf[t, pl.ds(mine, 1), 1, g : g + 1] = yi[None]

        def y_copy(i):
            return pltpu.make_async_remote_copy(
                ybuf.at[t, mine], ybuf.at[t, mine], y_ssem.at[t, i], y_rsem.at[t, i],
                device_id={"gb": lax.rem(mine + i, n_gb)}, device_id_type=MESH,
            )

        each(1, n_gb, lambda i: y_copy(i).start())
        each(1, n_gb, lambda i: y_copy(i).wait())
        yr = ybuf[t, 0, 0]
        yi = ybuf[t, 0, 1]
        for i in range(1, n_gb):
            yr = yr + ybuf[t, i, 0]
            yi = yi + ybuf[t, i, 1]
        field = pulse[t]
        dr = state[4] * ai + yi * g_scale - field * state[3]
        di = -(state[4] * ar + yr * g_scale - field * state[2])
        return dr, di

    ar = state[0]
    ai = state[1]
    dr, di = section(0, ar, ai)
    dr, di = section(1, ar + 0.5 * TIME_STEP * dr, ai + 0.5 * TIME_STEP * di)
    out[0] = ar + TIME_STEP * dr
    out[1] = ai + TIME_STEP * di


def body(amplitudes, pulse_field, pair_density, energies, dipoles, coulomb, screened, partners, shells, counts):
    k_rows, slots = partners.shape
    pairs = amplitudes.shape[2]
    g_local = coulomb.shape[0]
    n_kb = lax.axis_size("kb")
    n_gb = lax.axis_size("gb")
    groups = k_rows * pairs // 256
    width = -(-g_local // 256) * 256
    chunks = [256] * (width // 256)
    scales = (
        2.0 / math.sqrt(pairs * k_rows * n_kb),
        1.0 / math.sqrt(pairs * slots),
        1.0 / math.sqrt(g_local * n_gb),
    )
    state = jnp.concatenate([amplitudes, dipoles, energies[None]], axis=0).reshape(5, groups, 256)
    nch = len(chunks)
    vmem = pl.BlockSpec(memory_space=pltpu.VMEM)
    dma = pltpu.SemaphoreType.DMA
    result = pl.pallas_call(
        functools.partial(kernel, n_kb, n_gb, k_rows, pairs, slots, g_local, chunks, scales),
        out_shape=jax.ShapeDtypeStruct((2, groups, 256), F32),
        in_specs=[pl.BlockSpec(memory_space=pltpu.SMEM), vmem, pl.BlockSpec(memory_space=pl.ANY)] + [vmem] * 5,
        out_specs=vmem,
        scratch_shapes=[
            pltpu.VMEM(pair_density.shape, BF16),
            pltpu.VMEM((3, 8, LANES), F32),
            pltpu.VMEM((3, 8, LANES), F32),
            pltpu.VMEM((2, 2 * LANES, width), BF16),
            pltpu.VMEM((2, nch, 3, 2 * CAP, 256), BF16),
            pltpu.VMEM((2, nch, 4, 2 * CAP, 256), BF16),
            pltpu.VMEM((2, nch, n_kb, 2, 256), F32),
            pltpu.VMEM((2, n_gb, 2, groups, 256), F32),
            pltpu.VMEM((slots * 2 * k_rows, 8 * CAP), BF16),
            pltpu.VMEM((slots, k_rows, width), F32),
            pltpu.VMEM((screened.shape[0], width), F32),
            pltpu.VMEM((1, width), F32),
            dma((groups,)),
            dma((3,)),
            dma((3,)),
            dma((2, nch, 3)),
            dma((2, nch, 3)),
            dma((2, nch, n_kb)),
            dma((2, nch, n_kb)),
            dma((2, n_gb)),
            dma((2, n_gb)),
        ],
        compiler_params=pltpu.CompilerParams(
            collective_id=0, has_side_effects=True, vmem_limit_bytes=48 * 1024 * 1024
        ),
    )(
        pulse_field, state, pair_density, coulomb[None, :], screened, partners, shells, counts[:, None]
    )
    return result.reshape(2, k_rows, pairs)


def solution(mesh):
    in_specs = (
        P("grp", "kb", None),
        P("grp"),
        P(None, "kb", None, "gb"),
        P("kb", None),
        P(None, "kb", None),
        P("gb"),
        P(None, "gb"),
        P("kb", None),
        P("kb", None),
        P("kb"),
    )
    out_specs = P("grp", "kb", None)
    return jax.shard_map(body, mesh=mesh, in_specs=in_specs, out_specs=out_specs, check_vma=False)
```

```python
import functools
import math

import jax
import jax.numpy as jnp
from jax import lax
from jax.experimental import pallas as pl
from jax.experimental.pallas import tpu as pltpu
from jax.sharding import PartitionSpec as P

CAP = 24
TIME_STEP = 0.25
LANES = 128
MESH = pl.DeviceIdType.MESH
F32 = jnp.float32
BF16 = jnp.bfloat16


def iota(shape, dim):
    return lax.broadcasted_iota(jnp.int32, shape, dim)


def nn(a, b):
    return lax.dot_general(a, b, (((1,), (0,)), ((), ())), preferred_element_type=F32)


def nt(a, b):
    return lax.dot_general(a, b, (((1,), (1,)), ((), ())), preferred_element_type=F32)


def each(lo, hi, fn):
    if hi - lo <= 8:
        for i in range(lo, hi):
            fn(i)
    else:
        lax.fori_loop(lo, hi, lambda i, c: (fn(i), c)[1], 0)


def picks(rows4):
    wanted = jnp.concatenate(rows4 + rows4, axis=0)
    upper = (iota((LANES, LANES), 0) <= iota((LANES, LANES), 1)).astype(F32).astype(BF16)
    rank = nn(wanted.astype(BF16), upper)
    order = iota((2 * CAP, LANES), 0)
    order = jnp.where(order >= CAP, order - CAP, order).astype(F32) + 1.0
    blocks = []
    for s in range(4):
        hit = (rank[s : s + 1] == order).astype(F32) * wanted[s : s + 1]
        blocks.append(hit)
    return jnp.concatenate(blocks, axis=0)


def kernel(
    n_kb, n_gb, k_rows, pairs, slots, g_local, chunks, scales,
    pulse, amps_hbm, dens_hbm, energies_hbm, dipoles_hbm, coulomb_hbm, screened_hbm, partners_hbm, shells_hbm, counts_hbm,
    out,
    amps, energies, dipoles, coulomb, screened, partners, shells, counts, small_sem,
    dens, req_send, req_recv, zb, send, rows, nbuf, ybuf, onehot, weight, scr, coul,
    dens_sem, req_ssem, req_rsem, row_ssem, row_rsem, n_ssem, n_rsem, y_ssem, y_rsem,
):
    exchange_weight, direct_weight, g_scale = scales
    me = lax.axis_index("kb")
    mine = lax.axis_index("gb")
    groups = k_rows * pairs // 256
    per = 256 // pairs
    step = 2
    small = {}
    for i, (name, src, dst) in enumerate(
        (
            ("partners", partners_hbm, partners),
            ("amps", amps_hbm, amps),
            ("screened", screened_hbm, screened),
            ("shells", shells_hbm, shells),
            ("counts", counts_hbm, counts),
            ("coulomb", coulomb_hbm, coulomb),
            ("energies", energies_hbm, energies),
            ("dipoles", dipoles_hbm, dipoles),
        )
    ):
        small[name] = pltpu.make_async_copy(src, dst, small_sem.at[i])
        small[name].start()
    loads = []
    for i in range(groups // step):
        span = pl.ds(i * step * per, step * per)
        cp = pltpu.make_async_copy(dens_hbm.at[:, span], dens.at[:, span], dens_sem.at[i])
        cp.start()
        loads.append(cp)

    barrier = pltpu.get_barrier_semaphore()

    def greet_kb(i):
        pl.semaphore_signal(barrier, inc=1, device_id={"kb": lax.rem(me + i, n_kb)}, device_id_type=MESH)

    def greet_gb(i):
        pl.semaphore_signal(barrier, inc=1, device_id={"gb": lax.rem(mine + i, n_gb)}, device_id_type=MESH)

    each(1, n_kb, greet_kb)
    each(1, n_gb, greet_gb)

    span = n_kb * k_rows
    small["partners"].wait()
    rel = partners[...].T - me * k_rows
    rel = jnp.where(rel < 0, rel + span, rel)
    half_at = (n_kb // 2) * k_rows
    last_at = (n_kb - 1) * k_rows
    key = jnp.where(
        rel < k_rows,
        rel,
        jnp.where(
            rel >= last_at,
            rel - last_at + LANES,
            jnp.where(rel < 2 * k_rows, rel - k_rows + 2 * LANES, rel - half_at + 3 * LANES),
        ),
    )
    first = key[:, 0:1]
    mine4 = []
    for s in range(4):
        hit = (first == iota((k_rows, LANES), 1) + s * LANES).astype(F32)
        mine4.append(jnp.max(hit, axis=0, keepdims=True))
    for s in range(1, 4):
        req_send[s - 1] = jnp.broadcast_to(mine4[s], (8, LANES))

    pl.semaphore_wait(barrier, n_kb - 1 + n_gb - 1)

    sources = [None, lax.rem(me + n_kb - 1, n_kb), lax.rem(me + 1, n_kb), lax.rem(me + n_kb // 2, n_kb)]
    targets = [None, lax.rem(me + 1, n_kb), lax.rem(me + n_kb - 1, n_kb), lax.rem(me + n_kb // 2, n_kb)]
    reqs = []
    for s in range(1, 4):
        cp = pltpu.make_async_remote_copy(
            req_send.at[s - 1], req_recv.at[s - 1], req_ssem.at[s - 1], req_rsem.at[s - 1],
            device_id={"kb": sources[s]}, device_id_type=MESH,
        )
        cp.start()
        reqs.append(cp)

    own = picks(mine4)
    cols = 8 * CAP
    number = iota((8, LANES), 1).astype(F32).astype(BF16)
    at = iota((1, cols), 1)
    slot_at = (at >= 2 * CAP).astype(jnp.int32) + (at >= 4 * CAP).astype(jnp.int32) + (at >= 6 * CAP).astype(jnp.int32)
    imag_at = (at - slot_at * 2 * CAP >= CAP).astype(jnp.int32)
    wanted_key = nt(number, own.astype(BF16))[0:1].astype(jnp.int32) + slot_at * LANES
    scr[...] = jnp.zeros_like(scr)
    for name in ("screened", "coulomb", "shells", "counts"):
        small[name].wait()
    kind_of = shells[...].T
    live = jnp.broadcast_to(counts[...], (8, k_rows)).T[:, 0:1]
    scr[:, 0:g_local] = screened[...]
    coul[...] = jnp.zeros_like(coul)
    coul[:, 0:g_local] = coulomb[...] * exchange_weight
    zb[...] = jnp.zeros_like(zb)
    hi = scr[...].astype(BF16)
    rest = scr[...] - hi.astype(F32)
    mid = rest.astype(BF16)
    low = (rest - mid.astype(F32)).astype(BF16)
    kinds = screened.shape[0]
    for j in range(slots):
        hit = key[:, j : j + 1] == wanted_key
        onehot[j * 2 * k_rows : j * 2 * k_rows + k_rows] = (
            jnp.where(imag_at == 0, hit.astype(F32), 0.0).astype(BF16)
        )
        onehot[j * 2 * k_rows + k_rows : (j + 1) * 2 * k_rows] = (
            jnp.where(imag_at == 1, hit.astype(F32), 0.0).astype(BF16)
        )
        kind = (kind_of[:, j : j + 1] == iota((k_rows, kinds), 1)).astype(F32)
        kind = jnp.where(live > j, kind, 0.0).astype(BF16)
        weight[j] = nn(kind, hi) + (nn(kind, mid) + nn(kind, low))

    for cp in reqs:
        cp.wait()
    given = picks([mine4[0]] + [req_recv[s][0:1] for s in range(3)])
    row_at = iota((cols, 1), 0)
    row_slot = (row_at >= 2 * CAP).astype(jnp.int32) + (row_at >= 4 * CAP).astype(jnp.int32) + (row_at >= 6 * CAP).astype(jnp.int32)
    row_imag = row_at - row_slot * 2 * CAP >= CAP
    choose = jnp.concatenate(
        [jnp.where(row_imag, 0.0, given), jnp.where(row_imag, given, 0.0)], axis=1
    ).astype(BF16)

    diag = iota((per, 256), 1) // pairs == iota((per, 256), 0)
    starts = [sum(chunks[:i]) for i in range(len(chunks))]

    lane_pair = iota((pairs, 256), 1)
    spread = (lane_pair - lane_pair // pairs * pairs == iota((pairs, 256), 0)).astype(F32)
    spread = jnp.concatenate([spread] * 3, axis=0).astype(BF16)

    def flat(x):
        a = x.astype(BF16)
        b = x - a.astype(F32)
        c = b.astype(BF16)
        d = (b - c.astype(F32)).astype(BF16)
        parts = jnp.concatenate([a, c, d], axis=0)
        wide = lax.dot_general(parts, spread, (((0,), (0,)), ((), ())), preferred_element_type=F32)
        return jnp.concatenate(
            [
                jnp.sum(jnp.where(diag, wide[g * per : (g + 1) * per], 0.0), axis=0, keepdims=True)
                for g in range(groups)
            ],
            axis=0,
        )

    for name in ("amps", "energies", "dipoles"):
        small[name].wait()
    energy = flat(energies[...])
    dipole_r = flat(dipoles[0])
    dipole_i = flat(dipoles[1])

    def section(t, ar, ai):
        left, right = [], []
        for g in range(groups):
            br = jnp.where(diag, jnp.broadcast_to(ar[g : g + 1], (per, 256)), 0.0).astype(BF16)
            bi = jnp.where(diag, jnp.broadcast_to(ai[g : g + 1], (per, 256)), 0.0).astype(BF16)
            left.append(jnp.concatenate([br, bi], axis=0))
            right.append(jnp.concatenate([-bi, br], axis=0))
        row_copies = []
        n_copies = []
        for c, width in enumerate(chunks):
            lo = starts[c]
            real = min(width, g_local - lo)
            sr = jnp.zeros((1, real), F32)
            si = jnp.zeros((1, real), F32)
            for g in range(groups):
                if t == 0 and c == 0 and g % step == 0:
                    loads[g // step].wait()
                mr = dens[0, g * per : (g + 1) * per, :, lo : lo + real].reshape(256, real)
                mi = dens[1, g * per : (g + 1) * per, :, lo : lo + real].reshape(256, real)
                z = nn(left[g], mr) + nn(right[g], mi)
                sr = sr + jnp.sum(z[0:per], axis=0, keepdims=True)
                si = si + jnp.sum(z[per : 2 * per], axis=0, keepdims=True)
                zb[t, g * per : (g + 1) * per, lo : lo + real] = z[0:per].astype(BF16)
                zb[t, LANES + g * per : LANES + (g + 1) * per, lo : lo + real] = z[per : 2 * per].astype(BF16)
            if real < width:
                nbuf[t, c, pl.ds(me, 1)] = jnp.zeros((1, 2, width), F32)
            nbuf[t, c, pl.ds(me, 1), :, 0:real] = jnp.concatenate([sr, si], axis=0)[None]

            def n_copy(i, c=c):
                return pltpu.make_async_remote_copy(
                    nbuf.at[t, c, me], nbuf.at[t, c, me], n_ssem.at[t, c, i], n_rsem.at[t, c, i],
                    device_id={"kb": lax.rem(me + i, n_kb)}, device_id_type=MESH,
                )

            each(1, n_kb, lambda i: n_copy(i).start())
            n_copies.append(n_copy)
            picked = nn(choose, zb[t, :, lo : lo + width]).astype(BF16)
            started = []
            for s in range(1, 4):
                send[t, c, s - 1] = picked[s * 2 * CAP : (s + 1) * 2 * CAP]
            for s in (3, 1, 2):
                cp = pltpu.make_async_remote_copy(
                    send.at[t, c, s - 1], rows.at[t, c, s], row_ssem.at[t, c, s - 1], row_rsem.at[t, c, s - 1],
                    device_id={"kb": targets[s]}, device_id_type=MESH,
                )
                cp.start()
                started.append(cp)
            rows[t, c, 0] = picked[0 : 2 * CAP]
            row_copies.append(started)

        forces = []
        for c, width in enumerate(chunks):
            lo = starts[c]
            for cp in row_copies[c]:
                cp.wait()
            pulled = nn(onehot[...], rows[t, c].reshape(cols, width))
            sum_r = jnp.zeros((k_rows, width), F32)
            sum_i = jnp.zeros((k_rows, width), F32)
            for j in range(slots):
                w = weight[j, :, lo : lo + width]
                sum_r = sum_r + pulled[j * 2 * k_rows : j * 2 * k_rows + k_rows] * w
                sum_i = sum_i + pulled[j * 2 * k_rows + k_rows : (j + 1) * 2 * k_rows] * w
            each(1, n_kb, lambda i: n_copies[c](i).wait())
            total = lax.fori_loop(0, n_kb, lambda i, a: a + nbuf[t, c, i], jnp.zeros((2, width), F32))
            total = total * coul[:, lo : lo + width]
            forces.append(
                (
                    (total[0:1] - direct_weight * sum_r).astype(BF16),
                    (total[1:2] - direct_weight * sum_i).astype(BF16),
                )
            )

        for g in range(groups):
            y = jnp.zeros((2 * per, 256), F32)
            for c, width in enumerate(chunks):
                lo = starts[c]
                real = min(width, g_local - lo)
                fr = forces[c][0][g * per : (g + 1) * per, 0:real]
                fi = forces[c][1][g * per : (g + 1) * per, 0:real]
                mr = dens[0, g * per : (g + 1) * per, :, lo : lo + real].reshape(256, real)
                mi = dens[1, g * per : (g + 1) * per, :, lo : lo + real].reshape(256, real)
                y = y + nt(jnp.concatenate([fr, fi], axis=0), mr) + nt(jnp.concatenate([fi, -fr], axis=0), mi)
            yr = jnp.sum(jnp.where(diag, y[0:per], 0.0), axis=0, keepdims=True)
            yi = jnp.sum(jnp.where(diag, y[per : 2 * per], 0.0), axis=0, keepdims=True)
            ybuf[t, pl.ds(mine, 1), 0, g : g + 1] = yr[None]
            ybuf[t, pl.ds(mine, 1), 1, g : g + 1] = yi[None]

        def y_copy(i):
            return pltpu.make_async_remote_copy(
                ybuf.at[t, mine], ybuf.at[t, mine], y_ssem.at[t, i], y_rsem.at[t, i],
                device_id={"gb": lax.rem(mine + i, n_gb)}, device_id_type=MESH,
            )

        each(1, n_gb, lambda i: y_copy(i).start())
        each(1, n_gb, lambda i: y_copy(i).wait())
        yr = ybuf[t, 0, 0]
        yi = ybuf[t, 0, 1]
        for i in range(1, n_gb):
            yr = yr + ybuf[t, i, 0]
            yi = yi + ybuf[t, i, 1]
        field = pulse[t]
        dr = energy * ai + yi * g_scale - field * dipole_i
        di = -(energy * ar + yr * g_scale - field * dipole_r)
        return dr, di

    ar = flat(amps[0])
    ai = flat(amps[1])
    dr, di = section(0, ar, ai)
    dr, di = section(1, ar + 0.5 * TIME_STEP * dr, ai + 0.5 * TIME_STEP * di)
    out[0] = ar + TIME_STEP * dr
    out[1] = ai + TIME_STEP * di


def body(amplitudes, pulse_field, pair_density, energies, dipoles, coulomb, screened, partners, shells, counts):
    k_rows, slots = partners.shape
    pairs = amplitudes.shape[2]
    g_local = coulomb.shape[0]
    n_kb = lax.axis_size("kb")
    n_gb = lax.axis_size("gb")
    groups = k_rows * pairs // 256
    width = -(-g_local // 256) * 256
    chunks = [256] * (width // 256)
    scales = (
        2.0 / math.sqrt(pairs * k_rows * n_kb),
        1.0 / math.sqrt(pairs * slots),
        1.0 / math.sqrt(g_local * n_gb),
    )
    nch = len(chunks)
    vmem = pl.BlockSpec(memory_space=pltpu.VMEM)
    dma = pltpu.SemaphoreType.DMA
    result = pl.pallas_call(
        functools.partial(kernel, n_kb, n_gb, k_rows, pairs, slots, g_local, chunks, scales),
        out_shape=jax.ShapeDtypeStruct((2, groups, 256), F32),
        in_specs=[pl.BlockSpec(memory_space=pltpu.SMEM)] + [pl.BlockSpec(memory_space=pltpu.HBM)] * 9,
        out_specs=vmem,
        scratch_shapes=[
            pltpu.VMEM((2, pairs, k_rows), F32),
            pltpu.VMEM((pairs, k_rows), F32),
            pltpu.VMEM((2, pairs, k_rows), F32),
            pltpu.VMEM((1, g_local), F32),
            pltpu.VMEM(screened.shape, F32),
            pltpu.VMEM((slots, k_rows), jnp.int32),
            pltpu.VMEM((slots, k_rows), jnp.int32),
            pltpu.VMEM((1, k_rows), jnp.int32),
            dma((8,)),
            pltpu.VMEM(pair_density.shape, BF16),
            pltpu.VMEM((3, 8, LANES), F32),
            pltpu.VMEM((3, 8, LANES), F32),
            pltpu.VMEM((2, 2 * LANES, width), BF16),
            pltpu.VMEM((2, nch, 3, 2 * CAP, 256), BF16),
            pltpu.VMEM((2, nch, 4, 2 * CAP, 256), BF16),
            pltpu.VMEM((2, nch, n_kb, 2, 256), F32),
            pltpu.VMEM((2, n_gb, 2, groups, 256), F32),
            pltpu.VMEM((slots * 2 * k_rows, 8 * CAP), BF16),
            pltpu.VMEM((slots, k_rows, width), F32),
            pltpu.VMEM((screened.shape[0], width), F32),
            pltpu.VMEM((1, width), F32),
            dma((groups,)),
            dma((3,)),
            dma((3,)),
            dma((2, nch, 3)),
            dma((2, nch, 3)),
            dma((2, nch, n_kb)),
            dma((2, nch, n_kb)),
            dma((2, n_gb)),
            dma((2, n_gb)),
        ],
        compiler_params=pltpu.CompilerParams(
            collective_id=0, has_side_effects=True, vmem_limit_bytes=63 * 1024 * 1024
        ),
    )(
        pulse_field,
        jnp.transpose(amplitudes, (0, 2, 1)),
        pair_density,
        energies.T,
        jnp.transpose(dipoles, (0, 2, 1)),
        coulomb[None, :],
        screened,
        partners.T,
        shells.T,
        counts[None, :],
    )
    return result.reshape(2, k_rows, pairs)


def solution(mesh):
    in_specs = (
        P("grp", "kb", None),
        P("grp"),
        P(None, "kb", None, "gb"),
        P("kb", None),
        P(None, "kb", None),
        P("gb"),
        P(None, "gb"),
        P("kb", None),
        P("kb", None),
        P("kb"),
    )
    out_specs = P("grp", "kb", None)
    return jax.shard_map(body, mesh=mesh, in_specs=in_specs, out_specs=out_specs, check_vma=False)
```

```python
import functools
import math

import jax
import jax.numpy as jnp
from jax import lax
from jax.experimental import pallas as pl
from jax.experimental.pallas import tpu as pltpu
from jax.sharding import PartitionSpec as P

CAP = 24
TIME_STEP = 0.25
LANES = 128
MESH = pl.DeviceIdType.MESH
F32 = jnp.float32
BF16 = jnp.bfloat16


def iota(shape, dim):
    return lax.broadcasted_iota(jnp.int32, shape, dim)


def nn(a, b):
    return lax.dot_general(a, b, (((1,), (0,)), ((), ())), preferred_element_type=F32)


def nt(a, b):
    return lax.dot_general(a, b, (((1,), (1,)), ((), ())), preferred_element_type=F32)


def each(lo, hi, fn):
    if hi - lo <= 8:
        for i in range(lo, hi):
            fn(i)
    else:
        lax.fori_loop(lo, hi, lambda i, c: (fn(i), c)[1], 0)


def picks(rows4):
    wanted = jnp.concatenate(rows4 + rows4, axis=0)
    upper = (iota((LANES, LANES), 0) <= iota((LANES, LANES), 1)).astype(F32).astype(BF16)
    rank = nn(wanted.astype(BF16), upper)
    order = iota((2 * CAP, LANES), 0)
    order = jnp.where(order >= CAP, order - CAP, order).astype(F32) + 1.0
    blocks = []
    for s in range(4):
        hit = (rank[s : s + 1] == order).astype(F32) * wanted[s : s + 1]
        blocks.append(hit)
    return jnp.concatenate(blocks, axis=0)


def kernel(
    n_kb, n_gb, k_rows, pairs, slots, g_local, chunks, scales,
    pulse, amps_hbm, dens_hbm, energies_hbm, dipoles_hbm, coulomb_hbm, screened_hbm, partners_hbm, shells_hbm, counts_hbm,
    out,
    amps, energies, dipoles, coulomb, screened, partners, shells, counts, small_sem,
    dens, req_send, req_recv, zb, send, rows, nbuf, ybuf, onehot, weight, scr, coul,
    dens_sem, req_ssem, req_rsem, row_ssem, row_rsem, n_ssem, n_rsem, y_ssem, y_rsem,
):
    exchange_weight, direct_weight, g_scale = scales
    me = lax.axis_index("kb")
    mine = lax.axis_index("gb")
    groups = k_rows * pairs // 256
    per = 256 // pairs
    step = 2
    small = {}
    for i, (name, src, dst) in enumerate(
        (
            ("partners", partners_hbm, partners),
            ("amps", amps_hbm, amps),
            ("screened", screened_hbm, screened),
            ("shells", shells_hbm, shells),
            ("counts", counts_hbm, counts),
            ("coulomb", coulomb_hbm, coulomb),
            ("energies", energies_hbm, energies),
            ("dipoles", dipoles_hbm, dipoles),
        )
    ):
        small[name] = pltpu.make_async_copy(src, dst, small_sem.at[i])
        small[name].start()
    loads = []
    for i in range(groups // step):
        span = pl.ds(i * step * per, step * per)
        cp = pltpu.make_async_copy(dens_hbm.at[:, span], dens.at[:, span], dens_sem.at[i])
        cp.start()
        loads.append(cp)

    barrier = pltpu.get_barrier_semaphore()

    def greet_kb(i):
        pl.semaphore_signal(barrier, inc=1, device_id={"kb": lax.rem(me + i, n_kb)}, device_id_type=MESH)

    def greet_gb(i):
        pl.semaphore_signal(barrier, inc=1, device_id={"gb": lax.rem(mine + i, n_gb)}, device_id_type=MESH)

    each(1, n_kb, greet_kb)
    each(1, n_gb, greet_gb)

    span = n_kb * k_rows
    small["partners"].wait()
    rel = partners[...].T - me * k_rows
    rel = jnp.where(rel < 0, rel + span, rel)
    half_at = (n_kb // 2) * k_rows
    last_at = (n_kb - 1) * k_rows
    key = jnp.where(
        rel < k_rows,
        rel,
        jnp.where(
            rel >= last_at,
            rel - last_at + LANES,
            jnp.where(rel < 2 * k_rows, rel - k_rows + 2 * LANES, rel - half_at + 3 * LANES),
        ),
    )
    first = key[:, 0:1]
    mine4 = []
    for s in range(4):
        hit = (first == iota((k_rows, LANES), 1) + s * LANES).astype(F32)
        mine4.append(jnp.max(hit, axis=0, keepdims=True))
    for s in range(1, 4):
        req_send[s - 1] = jnp.broadcast_to(mine4[s], (8, LANES))

    diag = iota((per, 256), 1) // pairs == iota((per, 256), 0)
    starts = [sum(chunks[:i]) for i in range(len(chunks))]
    lane_pair = iota((pairs, 256), 1)
    spread = (lane_pair - lane_pair // pairs * pairs == iota((pairs, 256), 0)).astype(F32)
    spread = jnp.concatenate([spread] * 3, axis=0).astype(BF16)

    def flat(x):
        a = x.astype(BF16)
        b = x - a.astype(F32)
        c = b.astype(BF16)
        d = (b - c.astype(F32)).astype(BF16)
        parts = jnp.concatenate([a, c, d], axis=0)
        wide = lax.dot_general(parts, spread, (((0,), (0,)), ((), ())), preferred_element_type=F32)
        return jnp.concatenate(
            [
                jnp.sum(jnp.where(diag, wide[g * per : (g + 1) * per], 0.0), axis=0, keepdims=True)
                for g in range(groups)
            ],
            axis=0,
        )

    small["amps"].wait()
    ar = flat(amps[0])
    ai = flat(amps[1])
    zb[...] = jnp.zeros_like(zb)
    for t in range(2):
        for h in range(2):
            ybuf[t, h, pl.ds(mine, 1)] = jnp.zeros((1, 8, 256), F32)
        for c in range(len(chunks)):
            nbuf[t, c, pl.ds(me, 1)] = jnp.zeros((1, 2, 256), F32)

    pl.semaphore_wait(barrier, n_kb - 1 + n_gb - 1)

    sources = [None, lax.rem(me + n_kb - 1, n_kb), lax.rem(me + 1, n_kb), lax.rem(me + n_kb // 2, n_kb)]
    targets = [None, lax.rem(me + 1, n_kb), lax.rem(me + n_kb - 1, n_kb), lax.rem(me + n_kb // 2, n_kb)]
    late = []
    reqs = []
    for s in range(1, 4):
        cp = pltpu.make_async_remote_copy(
            req_send.at[s - 1], req_recv.at[s - 1], req_ssem.at[s - 1], req_rsem.at[s - 1],
            device_id={"kb": sources[s]}, device_id_type=MESH,
        )
        cp.start()
        reqs.append(cp)
        late.append(cp.wait_send)

    cols = 8 * CAP
    halves = [range(0, groups // 2), range(groups // 2, groups)]

    def block(part, g, c):
        lo = starts[c]
        real = min(chunks[c], g_local - lo)
        return dens[part, g * per : (g + 1) * per, :, lo : lo + real].reshape(256, real)

    def diagonal(row):
        return jnp.where(diag, jnp.broadcast_to(row, (per, 256)), 0.0).astype(BF16)

    def sides(xr, xi):
        out_sides = []
        for i in range(xr.shape[0]):
            br = diagonal(xr[i : i + 1])
            bi = diagonal(xi[i : i + 1])
            out_sides.append((jnp.concatenate([br, bi], axis=0), jnp.concatenate([-bi, br], axis=0)))
        return out_sides

    def densities(t, c, gs, factors):
        lo = starts[c]
        real = min(chunks[c], g_local - lo)
        total = [jnp.zeros((1, real), F32)] * 2
        for g, (left, right) in zip(gs, factors):
            if t == 0 and c == 0 and g % step == 0:
                loads[g // step].wait()
            z = nn(left, block(0, g, c)) + nn(right, block(1, g, c))
            for part in range(2):
                zp = z[part * per : (part + 1) * per]
                total[part] = total[part] + jnp.sum(zp, axis=0, keepdims=True)
                zb[t, part * LANES + g * per : part * LANES + (g + 1) * per, lo : lo + real] = zp.astype(BF16)
        return jnp.concatenate(total, axis=0)

    def n_copy(t, c, i):
        return pltpu.make_async_remote_copy(
            nbuf.at[t, c, me], nbuf.at[t, c, me], n_ssem.at[t, c, i], n_rsem.at[t, c, i],
            device_id={"kb": lax.rem(me + i, n_kb)}, device_id_type=MESH,
        )

    def send_n(t, c, total):
        nbuf[t, c, pl.ds(me, 1), :, 0 : total.shape[1]] = total[None]
        each(1, n_kb, lambda i: n_copy(t, c, i).start())
        late.append(lambda: each(1, n_kb, lambda i: n_copy(t, c, i).wait_send()))

    def send_rows(t, c, choose):
        lo = starts[c]
        picked = nn(choose, zb[t, :, lo : lo + chunks[c]]).astype(BF16)
        for s in range(1, 4):
            send[t, c, s - 1] = picked[s * 2 * CAP : (s + 1) * 2 * CAP]
        started = []
        for s in (3, 1, 2):
            cp = pltpu.make_async_remote_copy(
                send.at[t, c, s - 1], rows.at[t, c, s], row_ssem.at[t, c, s - 1], row_rsem.at[t, c, s - 1],
                device_id={"kb": targets[s]}, device_id_type=MESH,
            )
            cp.start()
            started.append(cp)
            late.append(cp.wait_send)
        rows[t, c, 0] = picked[0 : 2 * CAP]
        return started

    def y_copy(t, h, i):
        return pltpu.make_async_remote_copy(
            ybuf.at[t, h, mine], ybuf.at[t, h, mine], y_ssem.at[t, h, i], y_rsem.at[t, h, i],
            device_id={"gb": lax.rem(mine + i, n_gb)}, device_id_type=MESH,
        )

    def project(t, row_copies):
        ys = [None] * groups
        for c, width in enumerate(chunks):
            lo = starts[c]
            real = min(width, g_local - lo)
            for cp in row_copies[c]:
                cp.wait_recv()
            pulled = nn(onehot[...], rows[t, c].reshape(cols, width))
            sums = []
            for part in range(2):
                acc = jnp.zeros((k_rows, width), F32)
                for j in range(slots):
                    at = (2 * j + part) * k_rows
                    acc = acc + pulled[at : at + k_rows] * weight[j, :, lo : lo + width]
                sums.append(acc)
            each(1, n_kb, lambda i: n_copy(t, c, i).wait_recv())
            total = lax.fori_loop(0, n_kb, lambda i, a: a + nbuf[t, c, i], jnp.zeros((2, width), F32))
            total = total * coul[:, lo : lo + width]
            fr = (total[0:1] - direct_weight * sums[0]).astype(BF16)[:, 0:real]
            fi = (total[1:2] - direct_weight * sums[1]).astype(BF16)[:, 0:real]
            for h in range(2):
                for i, g in enumerate(halves[h]):
                    cut = slice(g * per, (g + 1) * per)
                    y = nt(jnp.concatenate([fr[cut], fi[cut]], axis=0), block(0, g, c))
                    y = y + nt(jnp.concatenate([fi[cut], -fr[cut]], axis=0), block(1, g, c))
                    ys[g] = y if c == 0 else ys[g] + y
                    if c == len(chunks) - 1:
                        for part in range(2):
                            row = jnp.where(diag, ys[g][part * per : (part + 1) * per], 0.0)
                            at = part * 4 + i
                            ybuf[t, h, pl.ds(mine, 1), at : at + 1] = jnp.sum(row, axis=0, keepdims=True)[None]
                if c == len(chunks) - 1:
                    each(1, n_gb, lambda i: y_copy(t, h, i).start())
                    late.append(lambda h=h: each(1, n_gb, lambda i: y_copy(t, h, i).wait_send()))

    def slope(t, h, xr, xi):
        each(1, n_gb, lambda i: y_copy(t, h, i).wait_recv())
        y = ybuf[t, h, 0]
        for i in range(1, n_gb):
            y = y + ybuf[t, h, i]
        y = y * g_scale
        cut = slice(halves[h][0], halves[h][-1] + 1)
        count = len(halves[h])
        field = pulse[t]
        dr = energy[cut] * xi[cut] + y[4 : 4 + count] - field * dipole_i[cut]
        di = -(energy[cut] * xr[cut] + y[0:count] - field * dipole_r[cut])
        return dr, di

    factors = sides(ar, ai)
    row_copies = []
    choose = None
    for c in range(len(chunks)):
        send_n(0, c, densities(0, c, range(groups), factors))
        if choose is None:
            for cp in reqs:
                cp.wait_recv()
            given = picks([mine4[0]] + [req_recv[s][0:1] for s in range(3)])
            row_at = iota((cols, 1), 0)
            row_slot = sum((row_at >= 2 * CAP * m).astype(jnp.int32) for m in (1, 2, 3))
            row_imag = row_at - row_slot * 2 * CAP >= CAP
            choose = jnp.concatenate(
                [jnp.where(row_imag, 0.0, given), jnp.where(row_imag, given, 0.0)], axis=1
            ).astype(BF16)
        row_copies.append(send_rows(0, c, choose))

    own = picks(mine4)
    number = iota((8, LANES), 1).astype(F32).astype(BF16)
    at = iota((1, cols), 1)
    slot_at = sum((at >= 2 * CAP * m).astype(jnp.int32) for m in (1, 2, 3))
    imag_at = (at - slot_at * 2 * CAP >= CAP).astype(jnp.int32)
    wanted_key = nt(number, own.astype(BF16))[0:1].astype(jnp.int32) + slot_at * LANES
    for name in ("screened", "coulomb", "shells", "counts", "energies", "dipoles"):
        small[name].wait()
    kind_of = shells[...].T
    live = jnp.broadcast_to(counts[...], (8, k_rows)).T[:, 0:1]
    scr[...] = jnp.zeros_like(scr)
    scr[:, 0:g_local] = screened[...]
    coul[...] = jnp.zeros_like(coul)
    coul[:, 0:g_local] = coulomb[...] * exchange_weight
    hi = scr[...].astype(BF16)
    rest = scr[...] - hi.astype(F32)
    mid = rest.astype(BF16)
    low = (rest - mid.astype(F32)).astype(BF16)
    levels = jnp.concatenate([hi, mid, low], axis=0)
    kinds = screened.shape[0]
    for j in range(slots):
        hit = (key[:, j : j + 1] == wanted_key).astype(F32)
        for part in range(2):
            at_row = (2 * j + part) * k_rows
            onehot[at_row : at_row + k_rows] = jnp.where(imag_at == part, hit, 0.0).astype(BF16)
        kind = (kind_of[:, j : j + 1] == iota((k_rows, kinds), 1)).astype(F32)
        kind = jnp.where(live > j, kind, 0.0).astype(BF16)
        weight[j] = nn(jnp.concatenate([kind] * 3, axis=1), levels)
    energy = flat(energies[...])
    dipole_r = flat(dipoles[0])
    dipole_i = flat(dipoles[1])

    project(0, row_copies)

    totals = [None] * len(chunks)
    row_copies = []
    half_r = []
    half_i = []
    for h in range(2):
        cut = slice(halves[h][0], halves[h][-1] + 1)
        dr, di = slope(0, h, ar, ai)
        half_r.append(ar[cut] + 0.5 * TIME_STEP * dr)
        half_i.append(ai[cut] + 0.5 * TIME_STEP * di)
        factors = sides(half_r[h], half_i[h])
        for c in range(len(chunks)):
            part_total = densities(1, c, halves[h], factors)
            if h == 0:
                totals[c] = part_total
            else:
                send_n(1, c, totals[c] + part_total)
                row_copies.append(send_rows(1, c, choose))
    hr = jnp.concatenate(half_r, axis=0)
    hi_amp = jnp.concatenate(half_i, axis=0)
    project(1, row_copies)
    for h in range(2):
        cut = slice(halves[h][0], halves[h][-1] + 1)
        dr, di = slope(1, h, hr, hi_amp)
        out[0, cut] = ar[cut] + TIME_STEP * dr
        out[1, cut] = ai[cut] + TIME_STEP * di
    for wait in late:
        wait()


def body(amplitudes, pulse_field, pair_density, energies, dipoles, coulomb, screened, partners, shells, counts):
    k_rows, slots = partners.shape
    pairs = amplitudes.shape[2]
    g_local = coulomb.shape[0]
    n_kb = lax.axis_size("kb")
    n_gb = lax.axis_size("gb")
    groups = k_rows * pairs // 256
    width = -(-g_local // 256) * 256
    chunks = [256] * (width // 256)
    scales = (
        2.0 / math.sqrt(pairs * k_rows * n_kb),
        1.0 / math.sqrt(pairs * slots),
        1.0 / math.sqrt(g_local * n_gb),
    )
    nch = len(chunks)
    vmem = pl.BlockSpec(memory_space=pltpu.VMEM)
    dma = pltpu.SemaphoreType.DMA
    result = pl.pallas_call(
        functools.partial(kernel, n_kb, n_gb, k_rows, pairs, slots, g_local, chunks, scales),
        out_shape=jax.ShapeDtypeStruct((2, groups, 256), F32),
        in_specs=[pl.BlockSpec(memory_space=pltpu.SMEM)] + [pl.BlockSpec(memory_space=pltpu.HBM)] * 9,
        out_specs=vmem,
        scratch_shapes=[
            pltpu.VMEM((2, pairs, k_rows), F32),
            pltpu.VMEM((pairs, k_rows), F32),
            pltpu.VMEM((2, pairs, k_rows), F32),
            pltpu.VMEM((1, g_local), F32),
            pltpu.VMEM(screened.shape, F32),
            pltpu.VMEM((slots, k_rows), jnp.int32),
            pltpu.VMEM((slots, k_rows), jnp.int32),
            pltpu.VMEM((1, k_rows), jnp.int32),
            dma((8,)),
            pltpu.VMEM(pair_density.shape, BF16),
            pltpu.VMEM((3, 8, LANES), F32),
            pltpu.VMEM((3, 8, LANES), F32),
            pltpu.VMEM((2, 2 * LANES, width), BF16),
            pltpu.VMEM((2, nch, 3, 2 * CAP, 256), BF16),
            pltpu.VMEM((2, nch, 4, 2 * CAP, 256), BF16),
            pltpu.VMEM((2, nch, n_kb, 2, 256), F32),
            pltpu.VMEM((2, 2, n_gb, 8, 256), F32),
            pltpu.VMEM((slots * 2 * k_rows, 8 * CAP), BF16),
            pltpu.VMEM((slots, k_rows, width), F32),
            pltpu.VMEM((screened.shape[0], width), F32),
            pltpu.VMEM((1, width), F32),
            dma((groups,)),
            dma((3,)),
            dma((3,)),
            dma((2, nch, 3)),
            dma((2, nch, 3)),
            dma((2, nch, n_kb)),
            dma((2, nch, n_kb)),
            dma((2, 2, n_gb)),
            dma((2, 2, n_gb)),
        ],
        compiler_params=pltpu.CompilerParams(
            collective_id=0, has_side_effects=True, vmem_limit_bytes=63 * 1024 * 1024
        ),
    )(
        pulse_field,
        jnp.transpose(amplitudes, (0, 2, 1)),
        pair_density,
        energies.T,
        jnp.transpose(dipoles, (0, 2, 1)),
        coulomb[None, :],
        screened,
        partners.T,
        shells.T,
        counts[None, :],
    )
    return result.reshape(2, k_rows, pairs)


def solution(mesh):
    in_specs = (
        P("grp", "kb", None),
        P("grp"),
        P(None, "kb", None, "gb"),
        P("kb", None),
        P(None, "kb", None),
        P("gb"),
        P(None, "gb"),
        P("kb", None),
        P("kb", None),
        P("kb"),
    )
    out_specs = P("grp", "kb", None)
    return jax.shard_map(body, mesh=mesh, in_specs=in_specs, out_specs=out_specs, check_vma=False)
```

```python
import functools
import math

import jax
import jax.numpy as jnp
from jax import lax
from jax.experimental import pallas as pl
from jax.experimental.pallas import tpu as pltpu
from jax.sharding import PartitionSpec as P

CAP = 24
TIME_STEP = 0.25
LANES = 128
MESH = pl.DeviceIdType.MESH
F32 = jnp.float32
BF16 = jnp.bfloat16


def iota(shape, dim):
    return lax.broadcasted_iota(jnp.int32, shape, dim)


def nn(a, b):
    return lax.dot_general(a, b, (((1,), (0,)), ((), ())), preferred_element_type=F32)


def nt(a, b):
    return lax.dot_general(a, b, (((1,), (1,)), ((), ())), preferred_element_type=F32)


def each(lo, hi, fn):
    if hi - lo <= 8:
        for i in range(lo, hi):
            fn(i)
    else:
        lax.fori_loop(lo, hi, lambda i, c: (fn(i), c)[1], 0)


def picks(rows4):
    wanted = jnp.concatenate(rows4 + rows4, axis=0)
    upper = (iota((LANES, LANES), 0) <= iota((LANES, LANES), 1)).astype(F32).astype(BF16)
    rank = nn(wanted.astype(BF16), upper)
    order = iota((2 * CAP, LANES), 0)
    order = jnp.where(order >= CAP, order - CAP, order).astype(F32) + 1.0
    blocks = []
    for s in range(4):
        hit = (rank[s : s + 1] == order).astype(F32) * wanted[s : s + 1]
        blocks.append(hit)
    return jnp.concatenate(blocks, axis=0)


def kernel(
    n_kb, n_gb, k_rows, pairs, slots, g_local, chunks, scales,
    pulse, amps_hbm, dens_hbm, energies_hbm, dipoles_hbm, coulomb_hbm, screened_hbm, partners_hbm, shells_hbm, counts_hbm,
    out,
    amps, energies, dipoles, coulomb, screened, partners, shells, counts, small_sem,
    dens, req_send, req_recv, zb, send, rows, nbuf, ybuf, onehot, weight, scr, coul,
    dens_sem, req_ssem, req_rsem, row_ssem, row_rsem, n_ssem, n_rsem, y_ssem, y_rsem,
):
    exchange_weight, direct_weight, g_scale = scales
    me = lax.axis_index("kb")
    mine = lax.axis_index("gb")
    groups = k_rows * pairs // 256
    per = 256 // pairs
    step = 2
    small = {}
    for i, (name, src, dst) in enumerate(
        (
            ("partners", partners_hbm, partners),
            ("amps", amps_hbm, amps),
            ("screened", screened_hbm, screened),
            ("shells", shells_hbm, shells),
            ("counts", counts_hbm, counts),
            ("coulomb", coulomb_hbm, coulomb),
            ("energies", energies_hbm, energies),
            ("dipoles", dipoles_hbm, dipoles),
        )
    ):
        small[name] = pltpu.make_async_copy(src, dst, small_sem.at[i])
        small[name].start()
    loads = []
    for i in range(groups // step):
        span = pl.ds(i * step * per, step * per)
        cp = pltpu.make_async_copy(dens_hbm.at[:, span], dens.at[:, span], dens_sem.at[i])
        cp.start()
        loads.append(cp)

    barrier = pltpu.get_barrier_semaphore()

    def greet_kb(i):
        pl.semaphore_signal(barrier, inc=1, device_id={"kb": lax.rem(me + i, n_kb)}, device_id_type=MESH)

    def greet_gb(i):
        pl.semaphore_signal(barrier, inc=1, device_id={"gb": lax.rem(mine + i, n_gb)}, device_id_type=MESH)

    each(1, n_kb, greet_kb)
    each(1, n_gb, greet_gb)

    span = n_kb * k_rows
    small["partners"].wait()
    rel = partners[...].T - me * k_rows
    rel = jnp.where(rel < 0, rel + span, rel)
    half_at = (n_kb // 2) * k_rows
    last_at = (n_kb - 1) * k_rows
    key = jnp.where(
        rel < k_rows,
        rel,
        jnp.where(
            rel >= last_at,
            rel - last_at + LANES,
            jnp.where(rel < 2 * k_rows, rel - k_rows + 2 * LANES, rel - half_at + 3 * LANES),
        ),
    )
    first = key[:, 0:1]
    mine4 = []
    for s in range(4):
        hit = (first == iota((k_rows, LANES), 1) + s * LANES).astype(F32)
        mine4.append(jnp.max(hit, axis=0, keepdims=True))
    for s in range(1, 4):
        req_send[s - 1] = jnp.broadcast_to(mine4[s], (8, LANES))

    diag = iota((per, 256), 1) // pairs == iota((per, 256), 0)
    starts = [sum(chunks[:i]) for i in range(len(chunks))]
    lane_pair = iota((pairs, 256), 1)
    spread = (lane_pair - lane_pair // pairs * pairs == iota((pairs, 256), 0)).astype(F32)
    spread = jnp.concatenate([spread] * 3, axis=0).astype(BF16)

    def flat(x):
        a = x.astype(BF16)
        b = x - a.astype(F32)
        c = b.astype(BF16)
        d = (b - c.astype(F32)).astype(BF16)
        parts = jnp.concatenate([a, c, d], axis=0)
        wide = lax.dot_general(parts, spread, (((0,), (0,)), ((), ())), preferred_element_type=F32)
        return jnp.concatenate(
            [
                jnp.sum(jnp.where(diag, wide[g * per : (g + 1) * per], 0.0), axis=0, keepdims=True)
                for g in range(groups)
            ],
            axis=0,
        )

    small["amps"].wait()
    ar = flat(amps[0])
    ai = flat(amps[1])
    zb[...] = jnp.zeros_like(zb)
    for t in range(2):
        ybuf[t, 0, pl.ds(mine, 1)] = jnp.zeros((1, 16, 256), F32)
        for c in range(len(chunks)):
            nbuf[t, c, pl.ds(me, 1)] = jnp.zeros((1, 2, 256), F32)

    pl.semaphore_wait(barrier, n_kb - 1 + n_gb - 1)

    sources = [None, lax.rem(me + n_kb - 1, n_kb), lax.rem(me + 1, n_kb), lax.rem(me + n_kb // 2, n_kb)]
    targets = [None, lax.rem(me + 1, n_kb), lax.rem(me + n_kb - 1, n_kb), lax.rem(me + n_kb // 2, n_kb)]
    late = []
    reqs = []
    for s in range(1, 4):
        cp = pltpu.make_async_remote_copy(
            req_send.at[s - 1], req_recv.at[s - 1], req_ssem.at[s - 1], req_rsem.at[s - 1],
            device_id={"kb": sources[s]}, device_id_type=MESH,
        )
        cp.start()
        reqs.append(cp)
        late.append(cp.wait_send)

    cols = 8 * CAP
    halves = [range(groups)]

    def block(part, g, c):
        lo = starts[c]
        real = min(chunks[c], g_local - lo)
        return dens[part, g * per : (g + 1) * per, :, lo : lo + real].reshape(256, real)

    def diagonal(row):
        return jnp.where(diag, jnp.broadcast_to(row, (per, 256)), 0.0).astype(BF16)

    def sides(xr, xi):
        out_sides = []
        for i in range(xr.shape[0]):
            br = diagonal(xr[i : i + 1])
            bi = diagonal(xi[i : i + 1])
            out_sides.append((jnp.concatenate([br, bi], axis=0), jnp.concatenate([-bi, br], axis=0)))
        return out_sides

    def densities(t, c, gs, factors):
        lo = starts[c]
        real = min(chunks[c], g_local - lo)
        total = [jnp.zeros((1, real), F32)] * 2
        for g, (left, right) in zip(gs, factors):
            if t == 0 and c == 0 and g % step == 0:
                loads[g // step].wait()
            z = nn(left, block(0, g, c)) + nn(right, block(1, g, c))
            for part in range(2):
                zp = z[part * per : (part + 1) * per]
                total[part] = total[part] + jnp.sum(zp, axis=0, keepdims=True)
                zb[t, part * LANES + g * per : part * LANES + (g + 1) * per, lo : lo + real] = zp.astype(BF16)
        return jnp.concatenate(total, axis=0)

    def n_copy(t, c, i):
        return pltpu.make_async_remote_copy(
            nbuf.at[t, c, me], nbuf.at[t, c, me], n_ssem.at[t, c, i], n_rsem.at[t, c, i],
            device_id={"kb": lax.rem(me + i, n_kb)}, device_id_type=MESH,
        )

    def send_n(t, c, total):
        nbuf[t, c, pl.ds(me, 1), :, 0 : total.shape[1]] = total[None]
        each(1, n_kb, lambda i: n_copy(t, c, i).start())
        late.append(lambda: each(1, n_kb, lambda i: n_copy(t, c, i).wait_send()))

    def send_rows(t, c, choose):
        lo = starts[c]
        picked = nn(choose, zb[t, :, lo : lo + chunks[c]]).astype(BF16)
        for s in range(1, 4):
            send[t, c, s - 1] = picked[s * 2 * CAP : (s + 1) * 2 * CAP]
        started = []
        for s in (3, 1, 2):
            cp = pltpu.make_async_remote_copy(
                send.at[t, c, s - 1], rows.at[t, c, s], row_ssem.at[t, c, s - 1], row_rsem.at[t, c, s - 1],
                device_id={"kb": targets[s]}, device_id_type=MESH,
            )
            cp.start()
            started.append(cp)
            late.append(cp.wait_send)
        rows[t, c, 0] = picked[0 : 2 * CAP]
        return started

    def y_copy(t, h, i):
        return pltpu.make_async_remote_copy(
            ybuf.at[t, h, mine], ybuf.at[t, h, mine], y_ssem.at[t, h, i], y_rsem.at[t, h, i],
            device_id={"gb": lax.rem(mine + i, n_gb)}, device_id_type=MESH,
        )

    def project(t, row_copies):
        ys = [None] * groups
        for c, width in enumerate(chunks):
            lo = starts[c]
            real = min(width, g_local - lo)
            for cp in row_copies[c]:
                cp.wait_recv()
            pulled = nn(onehot[...], rows[t, c].reshape(cols, width))
            sums = []
            for part in range(2):
                acc = jnp.zeros((k_rows, width), F32)
                for j in range(slots):
                    at = (2 * j + part) * k_rows
                    acc = acc + pulled[at : at + k_rows] * weight[j, :, lo : lo + width]
                sums.append(acc)
            each(1, n_kb, lambda i: n_copy(t, c, i).wait_recv())
            if n_kb <= 8:
                total = sum((nbuf[t, c, i] for i in range(1, n_kb)), nbuf[t, c, 0])
            else:
                total = lax.fori_loop(0, n_kb, lambda i, a: a + nbuf[t, c, i], jnp.zeros((2, width), F32))
            total = total * coul[:, lo : lo + width]
            fr = (total[0:1] - direct_weight * sums[0]).astype(BF16)[:, 0:real]
            fi = (total[1:2] - direct_weight * sums[1]).astype(BF16)[:, 0:real]
            for h in range(len(halves)):
                for i, g in enumerate(halves[h]):
                    cut = slice(g * per, (g + 1) * per)
                    y = nt(jnp.concatenate([fr[cut], fi[cut]], axis=0), block(0, g, c))
                    y = y + nt(jnp.concatenate([fi[cut], -fr[cut]], axis=0), block(1, g, c))
                    ys[g] = y if c == 0 else ys[g] + y
                    if c == len(chunks) - 1:
                        for part in range(2):
                            row = jnp.where(diag, ys[g][part * per : (part + 1) * per], 0.0)
                            at = part * 8 + i
                            ybuf[t, h, pl.ds(mine, 1), at : at + 1] = jnp.sum(row, axis=0, keepdims=True)[None]
                if c == len(chunks) - 1:
                    each(1, n_gb, lambda i: y_copy(t, h, i).start())
                    late.append(lambda h=h: each(1, n_gb, lambda i: y_copy(t, h, i).wait_send()))

    def slope(t, h, xr, xi):
        each(1, n_gb, lambda i: y_copy(t, h, i).wait_recv())
        y = ybuf[t, h, 0]
        for i in range(1, n_gb):
            y = y + ybuf[t, h, i]
        y = y * g_scale
        cut = slice(halves[h][0], halves[h][-1] + 1)
        count = len(halves[h])
        field = pulse[t]
        dr = energy[cut] * xi[cut] + y[8 : 8 + count] - field * dipole_i[cut]
        di = -(energy[cut] * xr[cut] + y[0:count] - field * dipole_r[cut])
        return dr, di

    factors = sides(ar, ai)
    row_copies = []
    for c in range(len(chunks)):
        send_n(0, c, densities(0, c, range(groups), factors))
    for cp in reqs:
        cp.wait_recv()
    given = picks([mine4[0]] + [req_recv[s][0:1] for s in range(3)])
    row_at = iota((cols, 1), 0)
    row_slot = sum((row_at >= 2 * CAP * m).astype(jnp.int32) for m in (1, 2, 3))
    row_imag = row_at - row_slot * 2 * CAP >= CAP
    choose = jnp.concatenate(
        [jnp.where(row_imag, 0.0, given), jnp.where(row_imag, given, 0.0)], axis=1
    ).astype(BF16)
    for c in range(len(chunks)):
        row_copies.append(send_rows(0, c, choose))

    own = picks(mine4)
    number = iota((8, LANES), 1).astype(F32).astype(BF16)
    at = iota((1, cols), 1)
    slot_at = sum((at >= 2 * CAP * m).astype(jnp.int32) for m in (1, 2, 3))
    imag_at = (at - slot_at * 2 * CAP >= CAP).astype(jnp.int32)
    wanted_key = nt(number, own.astype(BF16))[0:1].astype(jnp.int32) + slot_at * LANES
    for name in ("screened", "coulomb", "shells", "counts", "energies", "dipoles"):
        small[name].wait()
    kind_of = shells[...].T
    live = jnp.broadcast_to(counts[...], (8, k_rows)).T[:, 0:1]
    scr[...] = jnp.zeros_like(scr)
    scr[:, 0:g_local] = screened[...]
    coul[...] = jnp.zeros_like(coul)
    coul[:, 0:g_local] = coulomb[...] * exchange_weight
    hi = scr[...].astype(BF16)
    rest = scr[...] - hi.astype(F32)
    mid = rest.astype(BF16)
    low = (rest - mid.astype(F32)).astype(BF16)
    levels = jnp.concatenate([hi, mid, low], axis=0)
    kinds = screened.shape[0]
    for j in range(slots):
        hit = (key[:, j : j + 1] == wanted_key).astype(F32)
        for part in range(2):
            at_row = (2 * j + part) * k_rows
            onehot[at_row : at_row + k_rows] = jnp.where(imag_at == part, hit, 0.0).astype(BF16)
        kind = (kind_of[:, j : j + 1] == iota((k_rows, kinds), 1)).astype(F32)
        kind = jnp.where(live > j, kind, 0.0).astype(BF16)
        weight[j] = nn(jnp.concatenate([kind] * 3, axis=1), levels)
    energy = flat(energies[...])
    dipole_r = flat(dipoles[0])
    dipole_i = flat(dipoles[1])

    project(0, row_copies)

    totals = [None] * len(chunks)
    row_copies = []
    half_r = []
    half_i = []
    for h in range(len(halves)):
        cut = slice(halves[h][0], halves[h][-1] + 1)
        dr, di = slope(0, h, ar, ai)
        half_r.append(ar[cut] + 0.5 * TIME_STEP * dr)
        half_i.append(ai[cut] + 0.5 * TIME_STEP * di)
        factors = sides(half_r[h], half_i[h])
        for c in range(len(chunks)):
            part_total = densities(1, c, halves[h], factors)
            if h < len(halves) - 1:
                totals[c] = part_total
            else:
                row_copies.append(send_rows(1, c, choose))
                send_n(1, c, part_total if h == 0 else totals[c] + part_total)
    hr = jnp.concatenate(half_r, axis=0)
    hi_amp = jnp.concatenate(half_i, axis=0)
    project(1, row_copies)
    for h in range(len(halves)):
        cut = slice(halves[h][0], halves[h][-1] + 1)
        dr, di = slope(1, h, hr, hi_amp)
        out[0, cut] = ar[cut] + TIME_STEP * dr
        out[1, cut] = ai[cut] + TIME_STEP * di
    for wait in late:
        wait()


def body(amplitudes, pulse_field, pair_density, energies, dipoles, coulomb, screened, partners, shells, counts):
    k_rows, slots = partners.shape
    pairs = amplitudes.shape[2]
    g_local = coulomb.shape[0]
    n_kb = lax.axis_size("kb")
    n_gb = lax.axis_size("gb")
    groups = k_rows * pairs // 256
    width = -(-g_local // 256) * 256
    chunks = [256] * (width // 256)
    scales = (
        2.0 / math.sqrt(pairs * k_rows * n_kb),
        1.0 / math.sqrt(pairs * slots),
        1.0 / math.sqrt(g_local * n_gb),
    )
    nch = len(chunks)
    vmem = pl.BlockSpec(memory_space=pltpu.VMEM)
    dma = pltpu.SemaphoreType.DMA
    result = pl.pallas_call(
        functools.partial(kernel, n_kb, n_gb, k_rows, pairs, slots, g_local, chunks, scales),
        out_shape=jax.ShapeDtypeStruct((2, groups, 256), F32),
        in_specs=[pl.BlockSpec(memory_space=pltpu.SMEM)] + [pl.BlockSpec(memory_space=pltpu.HBM)] * 9,
        out_specs=vmem,
        scratch_shapes=[
            pltpu.VMEM((2, pairs, k_rows), F32),
            pltpu.VMEM((pairs, k_rows), F32),
            pltpu.VMEM((2, pairs, k_rows), F32),
            pltpu.VMEM((1, g_local), F32),
            pltpu.VMEM(screened.shape, F32),
            pltpu.VMEM((slots, k_rows), jnp.int32),
            pltpu.VMEM((slots, k_rows), jnp.int32),
            pltpu.VMEM((1, k_rows), jnp.int32),
            dma((8,)),
            pltpu.VMEM(pair_density.shape, BF16),
            pltpu.VMEM((3, 8, LANES), F32),
            pltpu.VMEM((3, 8, LANES), F32),
            pltpu.VMEM((2, 2 * LANES, width), BF16),
            pltpu.VMEM((2, nch, 3, 2 * CAP, 256), BF16),
            pltpu.VMEM((2, nch, 4, 2 * CAP, 256), BF16),
            pltpu.VMEM((2, nch, n_kb, 2, 256), F32),
            pltpu.VMEM((2, 1, n_gb, 16, 256), F32),
            pltpu.VMEM((slots * 2 * k_rows, 8 * CAP), BF16),
            pltpu.VMEM((slots, k_rows, width), F32),
            pltpu.VMEM((screened.shape[0], width), F32),
            pltpu.VMEM((1, width), F32),
            dma((groups,)),
            dma((3,)),
            dma((3,)),
            dma((2, nch, 3)),
            dma((2, nch, 3)),
            dma((2, nch, n_kb)),
            dma((2, nch, n_kb)),
            dma((2, 2, n_gb)),
            dma((2, 2, n_gb)),
        ],
        compiler_params=pltpu.CompilerParams(
            collective_id=0, has_side_effects=True, vmem_limit_bytes=63 * 1024 * 1024
        ),
    )(
        pulse_field,
        jnp.transpose(amplitudes, (0, 2, 1)),
        pair_density,
        energies.T,
        jnp.transpose(dipoles, (0, 2, 1)),
        coulomb[None, :],
        screened,
        partners.T,
        shells.T,
        counts[None, :],
    )
    return result.reshape(2, k_rows, pairs)


def solution(mesh):
    in_specs = (
        P("grp", "kb", None),
        P("grp"),
        P(None, "kb", None, "gb"),
        P("kb", None),
        P(None, "kb", None),
        P("gb"),
        P(None, "gb"),
        P("kb", None),
        P("kb", None),
        P("kb"),
    )
    out_specs = P("grp", "kb", None)
    return jax.shard_map(body, mesh=mesh, in_specs=in_specs, out_specs=out_specs, check_vma=False)
```
